32 devices in a mesh: depth: 4 (over y, x), gx: 8 (over z, core).
Axes of the slice: x: 2, y: 2, z: 4, core: 2. Of those that a mesh axis runs over, the one named last changes fastest.
Arguments:
- offset_image: bfloat16 [64, 64, 32, 256], P(None, 'depth', 'gx'), may hold values from -6 to 6
- dip_class: int32 [64, 32, 256], P('depth', 'gx'), may hold values from 0 to 7
- slant_taper: bfloat16 [64, 64, 33], replicated, may hold values from -0.3125 to 0.3125
- band_offsets: int32 [64], replicated, may hold values from -14 to 14
- coefficients: float32 [8, 27], replicated, may hold values from -1.25 to 1.25
Outputs:
- smoothed: bfloat16 [64, 64, 32, 256], P(None, 'depth', 'gx')
The draws below stay inside these ranges and needn't reach their ends.
All inputs are finite; a program needn't handle non-finite values.
Results may differ from the reference program's by a relative error of at most 0.0049.
Values may be sent and summed in bfloat16 or wider, within the bound.
A program may use at most 64 MiB of HBM per device.

```python
import jax
import jax.numpy as jnp
from jax import lax

H = 64
ANG = 64
R = 16
BAND = 2
RX = 4
RY = 1
NQ = 8
NY = 256
TAPS = 27
NZ = 64
NX = 32


def place_ends(array, rng, low, largest):
    extent = array.shape
    spot = [jax.random.randint(jax.random.fold_in(rng, axis), (), 0, extent[axis]) for axis in range(len(extent))]
    array = array.at[tuple(spot)].set(low)
    longest = extent.index(max(extent))
    spot[longest] = (spot[longest] + 1) % extent[longest]
    return array.at[tuple(spot)].set(largest)


def levels(own_key, extent, cuts, low, top_value):
    factor_of = 1.0
    for dim, blocks in cuts:
        draws = jax.random.uniform(jax.random.fold_in(jax.random.fold_in(own_key, 6), dim), (blocks,), jnp.float32, low / len(cuts), top_value / len(cuts))
        factor_of = factor_of * jnp.repeat(jnp.exp(draws), extent[dim] // blocks).reshape((-1,) + (1,) * (len(extent) - 1 - dim))
    return factor_of


def bell_draw(key, shape, spread, reach, shards=(), kind=jnp.bfloat16):
    array = jax.random.normal(key, shape, jnp.float32) * spread
    if len(shards) > 0:
        array = levels(key, shape, shards, -0.22, 0.18) * array
    return jnp.clip(array, min=-reach, max=reach).astype(kind)


def setup_inputs(seed: int = 0) -> dict:
    arg_keys = jax.random.split(jax.random.key(seed), 6)
    return {
        "offset_image": bell_draw(arg_keys[0], (H, NZ, NX, NY), 1.0, 6.0, ((1, 4), (2, 8))),
        "dip_class": place_ends(jax.random.randint(arg_keys[1], (NZ, NX, NY), 0, NQ), jax.random.fold_in(arg_keys[1], 1), 0, NQ - 1).astype(jnp.int32),
        "slant_taper": bell_draw(arg_keys[2], (ANG, H, 2 * R + 1), (H * (2 * BAND + 1)) ** -0.5, 0.3125),
        "band_offsets": place_ends(jax.random.randint(arg_keys[3], (ANG,), BAND - R, R - BAND + 1), jax.random.fold_in(arg_keys[3], 1), BAND - R, R - BAND).astype(jnp.int32),
        "coefficients": bell_draw(arg_keys[4], (NQ, TAPS), TAPS ** -0.5, 1.25, (), jnp.float32),
    }


def slant_matrix_of(slant_taper, band_offsets, offset_count):
    offset_index = jnp.arange(offset_count, dtype=jnp.int32)
    depth_shift = jnp.floor_divide(band_offsets[:, None] * offset_index[None, :], offset_count)
    reach_index = jnp.arange(slant_taper.shape[2], dtype=jnp.int32) - R
    inside_band = jnp.abs(reach_index[None, None, :] - depth_shift[:, :, None]) <= BAND
    return jnp.where(inside_band, slant_taper, jnp.zeros_like(slant_taper))


def reference(offset_image, dip_class, slant_taper, band_offsets, coefficients):
    slant_matrix = slant_matrix_of(slant_taper, band_offsets, H).astype(jnp.float32)
    padded = jnp.pad(offset_image, ((0, 0), (R, R), (0, 0), (0, 0)))

    def one_depth(depth_level):
        window = lax.dynamic_slice_in_dim(padded, depth_level, 2 * R + 1, 1).astype(jnp.float32)
        return jnp.einsum("ahd,hdxy->axy", slant_matrix, window).astype(jnp.bfloat16)

    gathers = jnp.moveaxis(lax.map(one_depth, jnp.arange(NZ, dtype=jnp.int32)), 0, 1)
    tap_weights = jnp.moveaxis(jnp.take(coefficients, dip_class, axis=0), 3, 0)
    widened = jnp.pad(gathers, ((0, 0), (0, 0), (RX, RX), (RY, RY)))

    def smooth_angle(angle_plane):
        running = jnp.zeros((NZ, NX, NY), jnp.float32)
        for column_step in range(2 * RX + 1):
            for row_step in range(2 * RY + 1):
                tap_index = column_step * (2 * RY + 1) + row_step
                shifted = angle_plane[:, column_step:column_step + NX, row_step:row_step + NY]
                running = running + tap_weights[tap_index] * shifted.astype(jnp.float32)
        return running.astype(jnp.bfloat16)

    return lax.map(smooth_angle, widened)
```

```python
import functools

import jax
import jax.numpy as jnp
from jax import lax
from jax.experimental import pallas as pl
from jax.experimental.pallas import tpu as pltpu
from jax.sharding import PartitionSpec as P

R = 16
BAND = 2
RX = 4
RY = 1
COLS = 2
ALIGN = 8


def first_offsets(offset_count):
    steep = R - BAND
    above, below = [], []
    for distance in range(1, R + 1):
        up = [h for h in range(offset_count) if -(-steep * h // offset_count) + BAND >= distance]
        down = [h for h in range(offset_count) if steep * h // offset_count + BAND >= distance]
        above.append((up[0] if up else offset_count) // ALIGN * ALIGN)
        below.append((down[0] if down else offset_count) // ALIGN * ALIGN)
    return above, below


def slant_matrix_of(slant_taper, band_offsets, offset_count):
    offset_index = jnp.arange(offset_count, dtype=jnp.int32)
    depth_shift = jnp.floor_divide(band_offsets[:, None] * offset_index[None, :], offset_count)
    reach_index = jnp.arange(slant_taper.shape[2], dtype=jnp.int32) - R
    inside_band = jnp.abs(reach_index[None, None, :] - depth_shift[:, :, None]) <= BAND
    return jnp.where(inside_band, slant_taper, jnp.zeros_like(slant_taper))


def stack_matrices(slant_matrix, depth_cells, above, below):
    angles, offset_count, reach = slant_matrix.shape
    flat = jnp.swapaxes(slant_matrix, 1, 2).reshape(angles, reach * offset_count)
    rows = [
        jnp.pad(flat, ((0, 0), (z * offset_count, (depth_cells - 1 - z) * offset_count)))
        for z in range(depth_cells)
    ]
    whole = jnp.concatenate(rows, axis=0)
    pieces = []
    for row in range(R):
        start = above[R - 1 - row]
        if start < offset_count:
            pieces.append(whole[:, row * offset_count + start : (row + 1) * offset_count])
    pieces.append(whole[:, R * offset_count : (R + depth_cells) * offset_count])
    for row in range(R):
        start = below[row]
        first = (R + depth_cells + row) * offset_count
        if start < offset_count:
            pieces.append(whole[:, first + start : first + offset_count])
    return jnp.concatenate(pieces, axis=1)


def stack_kernel(matrix_ref, above_ref, own_ref, below_ref, out_ref):
    na, no = above_ref.shape[1], own_ref.shape[1]
    total = jnp.dot(matrix_ref[:, :na], above_ref[0], preferred_element_type=jnp.float32)
    total += jnp.dot(matrix_ref[:, na : na + no], own_ref[0], preferred_element_type=jnp.float32)
    total += jnp.dot(matrix_ref[:, na + no :], below_ref[0], preferred_element_type=jnp.float32)
    out_ref[0] = total.astype(out_ref.dtype)


def slant_stack(matrix, above, own, below):
    columns, _, cross = own.shape
    rows, depth = matrix.shape
    tile = 256 if rows % 256 == 0 else rows
    return pl.pallas_call(
        stack_kernel,
        grid=(rows // tile, columns),
        in_specs=[
            pl.BlockSpec((tile, depth), lambda m, c: (m, 0)),
            pl.BlockSpec((1, above.shape[1], cross), lambda m, c: (c, 0, 0)),
            pl.BlockSpec((1, own.shape[1], cross), lambda m, c: (c, 0, 0)),
            pl.BlockSpec((1, below.shape[1], cross), lambda m, c: (c, 0, 0)),
        ],
        out_specs=pl.BlockSpec((1, tile, cross), lambda m, c: (c, m, 0)),
        out_shape=jax.ShapeDtypeStruct((columns, rows, cross), jnp.bfloat16),
        compiler_params=pltpu.CompilerParams(vmem_limit_bytes=32 * 1024 * 1024),
        cost_estimate=pl.CostEstimate(
            flops=2 * rows * depth * columns * cross,
            bytes_accessed=2 * (rows * depth + columns * (depth + rows) * cross),
            transcendentals=0,
        ),
        name="slant_stack",
    )(matrix, above, own, below)


def smooth_kernel(lateral, chunks, weight_ref, *refs):
    ins, out_ref = refs[:-1], refs[-1]
    angles, cross = out_ref.shape[2:]
    step = 32 if angles % 32 == 0 else angles
    for x in range(lateral):
        for first in range(0, angles, step):
            sums = [None] * (2 * RY + 1)
            for i in range(2 * RX + 1):
                chunk, column = chunks[x + i]
                plane = ins[chunk][column, 0, first : first + step, :].astype(jnp.float32)
                for j in range(2 * RY + 1):
                    tap = i * (2 * RY + 1) + j
                    term = weight_ref[0, x, tap : tap + 1, :] * plane
                    sums[j] = term if sums[j] is None else sums[j] + term
            total = sums[RY]
            for j in range(2 * RY + 1):
                if j != RY:
                    total = total + pltpu.roll(sums[j], (RY - j) % cross, 1)
            out_ref[x, 0, first : first + step, :] = total.astype(out_ref.dtype)


def smooth(weights, parts, chunks, lateral, depth_cells, angles):
    cross = weights.shape[-1]
    parts = [p.reshape(p.shape[0], depth_cells, angles, cross) for p in parts]
    return pl.pallas_call(
        functools.partial(smooth_kernel, lateral, chunks),
        grid=(depth_cells,),
        in_specs=[pl.BlockSpec((1,) + weights.shape[1:], lambda z: (z, 0, 0, 0))]
        + [pl.BlockSpec((p.shape[0], 1, angles, cross), lambda z: (0, z, 0, 0)) for p in parts],
        out_specs=pl.BlockSpec((lateral, 1, angles, cross), lambda z: (0, z, 0, 0)),
        out_shape=jax.ShapeDtypeStruct((lateral, depth_cells, angles, cross), jnp.bfloat16),
        compiler_params=pltpu.CompilerParams(vmem_limit_bytes=32 * 1024 * 1024),
        cost_estimate=pl.CostEstimate(
            flops=54 * lateral * depth_cells * angles * cross,
            bytes_accessed=8 * lateral * depth_cells * angles * cross,
            transcendentals=0,
        ),
        name="smooth",
    )(weights, *parts)


def dip_weights(dip_class, coefficients):
    classes, taps = coefficients.shape
    cross = dip_class.shape[-1]
    width = 2 * RY + 1
    padded = jnp.pad(dip_class, ((0, 0), (0, 0), (2 * RY, 2 * RY)), constant_values=-1)
    moved = jnp.stack(
        [padded[:, :, 3 * RY - j : 3 * RY - j + cross] for j in range(width)]
    )
    class_index = jnp.arange(classes, dtype=jnp.int32)
    onehot = (moved[:, :, :, None] == class_index[:, None]).astype(jnp.float32)
    weights = jnp.einsum(
        "qij,jzxqy->zxijy",
        coefficients.reshape(classes, taps // width, width),
        onehot,
        precision=lax.Precision.HIGHEST,
    )
    return weights.reshape(weights.shape[:2] + (taps, cross))


def neighbours(axis):
    count = lax.axis_size(axis)
    up = [(i, i + 1) for i in range(count - 1)]
    return up, [(j, i) for i, j in up]


def local(offset_image, dip_class, slant_taper, band_offsets, coefficients):
    offset_count, depth_cells, lateral, cross = offset_image.shape
    angles = slant_taper.shape[0]
    above, below = first_offsets(offset_count)
    up, down = neighbours("depth")
    right, left = neighbours("gx")
    cols = COLS if lateral % COLS == 0 else lateral

    by_column = jnp.transpose(offset_image, (2, 1, 0, 3))
    halos = []
    for first in range(0, lateral, cols):
        part = by_column[first : first + cols]
        last = [
            part[:, depth_cells - R + row, above[R - 1 - row] :]
            for row in range(R)
            if above[R - 1 - row] < offset_count
        ]
        leading = [part[:, row, below[row] :] for row in range(R) if below[row] < offset_count]
        halos.append(
            (
                lax.ppermute(jnp.concatenate(last, axis=1), "depth", up),
                lax.ppermute(jnp.concatenate(leading, axis=1), "depth", down),
            )
        )
    matrix = stack_matrices(
        slant_matrix_of(slant_taper, band_offsets, offset_count), depth_cells, above, below
    )
    weights = dip_weights(dip_class, coefficients)
    own = by_column.reshape(lateral, depth_cells * offset_count, cross)
    mine, before, after = [], [], []
    for index, (upper, lower) in enumerate(halos):
        first = index * cols
        part = slant_stack(matrix, upper, own[first : first + cols], lower)
        mine.append(part)
        before.append(lax.ppermute(part, "gx", right))
        after.append(lax.ppermute(part, "gx", left))
    parts = before + mine + after
    chunks = [(p, c) for p in range(len(parts)) for c in range(cols)]
    chunks = chunks[lateral - RX : 2 * lateral + RX]
    out = smooth(weights, parts, chunks, lateral, depth_cells, angles)
    return jnp.transpose(out, (2, 1, 0, 3))


def solution(mesh):
    return jax.shard_map(
        local,
        mesh=mesh,
        in_specs=(P(None, "depth", "gx", None), P("depth", "gx", None), P(), P(), P()),
        out_specs=P(None, "depth", "gx", None),
        check_vma=False,
    )
```

```python
import functools

import jax
import jax.numpy as jnp
from jax import lax
from jax.experimental import pallas as pl
from jax.experimental.pallas import tpu as pltpu
from jax.sharding import PartitionSpec as P

R = 16
BAND = 2
RX = 4
RY = 1
COLS = 2
GROUP = 4
ALIGN = 8


def first_offsets(offset_count):
    steep = R - BAND
    above, below = [], []
    for distance in range(1, R + 1):
        up = [h for h in range(offset_count) if -(-steep * h // offset_count) + BAND >= distance]
        down = [h for h in range(offset_count) if steep * h // offset_count + BAND >= distance]
        above.append((up[0] if up else offset_count) // ALIGN * ALIGN)
        below.append((down[0] if down else offset_count) // ALIGN * ALIGN)
    return above, below


def slant_matrix_of(slant_taper, band_offsets, offset_count):
    offset_index = jnp.arange(offset_count, dtype=jnp.int32)
    depth_shift = jnp.floor_divide(band_offsets[:, None] * offset_index[None, :], offset_count)
    reach_index = jnp.arange(slant_taper.shape[2], dtype=jnp.int32) - R
    inside_band = jnp.abs(reach_index[None, None, :] - depth_shift[:, :, None]) <= BAND
    return jnp.where(inside_band, slant_taper, jnp.zeros_like(slant_taper))


def stack_matrix(slant_matrix, group):
    angles, offset_count, reach = slant_matrix.shape
    flat = jnp.swapaxes(slant_matrix, 1, 2).reshape(angles, reach * offset_count)
    rows = [
        jnp.pad(flat, ((0, 0), (z * offset_count, (group - 1 - z) * offset_count)))
        for z in range(group)
    ]
    return jnp.concatenate(rows, axis=0)


def packed_rows(starts, offset_count):
    rows, place = [], 0
    for row, start in enumerate(starts):
        if start < offset_count:
            rows.append((row, start, place))
            place += offset_count - start
    return rows, place


def pack_kernel(upper, lower, image_ref, last_ref, leading_ref):
    depth_cells, offset_count = image_ref.shape[1:3]
    for row, start, place in upper:
        last_ref[0, place : place + offset_count - start, :] = image_ref[
            0, depth_cells - R + row, start:, :
        ]
    for row, start, place in lower:
        leading_ref[0, place : place + offset_count - start, :] = image_ref[0, row, start:, :]


def pack(by_column, upper, lower):
    columns, depth_cells, offset_count, cross = by_column.shape
    sizes = [upper[1], lower[1]]
    return pl.pallas_call(
        functools.partial(pack_kernel, upper[0], lower[0]),
        grid=(columns,),
        in_specs=[pl.BlockSpec((1, depth_cells, offset_count, cross), lambda c: (c, 0, 0, 0))],
        out_specs=[pl.BlockSpec((1, n, cross), lambda c: (c, 0, 0)) for n in sizes],
        out_shape=[jax.ShapeDtypeStruct((columns, n, cross), jnp.bfloat16) for n in sizes],
        compiler_params=pltpu.CompilerParams(vmem_limit_bytes=32 * 1024 * 1024),
        cost_estimate=pl.CostEstimate(
            flops=0, bytes_accessed=4 * columns * sum(sizes) * cross, transcendentals=0
        ),
        name="pack",
    )(by_column)


def stack_kernel(upper, lower, group, matrix_ref, above_ref, own_ref, below_ref, out_ref, planes):
    depth_cells, offset_count, cross = own_ref.shape[1:]
    below_row = R + depth_cells

    @pl.when(pl.program_id(0) == 0)
    def _():
        planes[: R * offset_count, :] = jnp.zeros((R * offset_count, cross), planes.dtype)
        planes[below_row * offset_count :, :] = jnp.zeros((R * offset_count, cross), planes.dtype)

    for row, start, place in upper:
        planes[row * offset_count + start : (row + 1) * offset_count, :] = above_ref[
            0, place : place + offset_count - start, :
        ]
    for row in range(depth_cells):
        planes[(R + row) * offset_count : (R + row + 1) * offset_count, :] = own_ref[0, row]
    for row, start, place in lower:
        first = (below_row + row) * offset_count
        planes[first + start : first + offset_count, :] = below_ref[
            0, place : place + offset_count - start, :
        ]
    tile, depth = matrix_ref.shape
    for z in range(0, depth_cells, group):
        total = jnp.dot(
            matrix_ref[...],
            planes[z * offset_count : z * offset_count + depth, :],
            preferred_element_type=jnp.float32,
        )
        out_ref[0, z // group * tile : (z // group + 1) * tile, :] = total.astype(out_ref.dtype)


def slant_stack(matrix, group, above, by_column, below, upper, lower, first, columns):
    _, depth_cells, offset_count, cross = by_column.shape
    tile, depth = matrix.shape
    rows = depth_cells // group * tile
    return pl.pallas_call(
        functools.partial(stack_kernel, upper[0], lower[0], group),
        grid=(columns,),
        in_specs=[
            pl.BlockSpec((tile, depth), lambda c: (0, 0)),
            pl.BlockSpec((1, upper[1], cross), lambda c: (c, 0, 0)),
            pl.BlockSpec((1, depth_cells, offset_count, cross), lambda c: (c + first, 0, 0, 0)),
            pl.BlockSpec((1, lower[1], cross), lambda c: (c, 0, 0)),
        ],
        out_specs=pl.BlockSpec((1, rows, cross), lambda c: (c, 0, 0)),
        out_shape=jax.ShapeDtypeStruct((columns, rows, cross), jnp.bfloat16),
        scratch_shapes=[pltpu.VMEM(((2 * R + depth_cells) * offset_count, cross), jnp.bfloat16)],
        compiler_params=pltpu.CompilerParams(vmem_limit_bytes=32 * 1024 * 1024),
        cost_estimate=pl.CostEstimate(
            flops=2 * rows * depth * columns * cross,
            bytes_accessed=2 * (tile * depth + columns * (depth + rows) * cross),
            transcendentals=0,
        ),
        name="slant_stack",
    )(matrix, above, by_column, below)


def smooth_kernel(sources, weight_ref, *refs):
    out_ref = refs[-1]
    lateral, _, angles, cross = out_ref.shape
    step = 32 if angles % 32 == 0 else angles
    count = 1 + max(which for planes in sources for _, which, _ in planes)
    for x in range(lateral):
        for first in range(0, angles, step):
            sums = [None] * (2 * RY + 1)
            for i, which, column in sources[x]:
                plane = refs[which][column, 0, first : first + step, :].astype(jnp.float32)
                for j in range(2 * RY + 1):
                    tap = i * (2 * RY + 1) + j
                    term = weight_ref[0, x, tap : tap + 1, :] * plane
                    sums[j] = term if sums[j] is None else sums[j] + term
            total = sums[RY]
            for j in range(2 * RY + 1):
                if j != RY:
                    total = total + pltpu.roll(sums[j], (RY - j) % cross, 1)
            if len(refs) > count + 1:
                total = total + refs[count][x, 0, first : first + step, :]
            out_ref[x, 0, first : first + step, :] = total.astype(out_ref.dtype)


def smooth(weights, parts, sources, partial, lateral, depth_cells, angles, kind):
    cross = weights.shape[-1]
    used = sorted({which for planes in sources for _, which, _ in planes})
    sources = [[(i, used.index(which), column) for i, which, column in planes] for planes in sources]
    ins = [parts[which] for which in used]
    ins = [p.reshape(p.shape[0], depth_cells, angles, cross) for p in ins]
    if partial is not None:
        ins.append(partial)
    planes = sum(len(s) for s in sources)
    return pl.pallas_call(
        functools.partial(smooth_kernel, sources),
        grid=(depth_cells,),
        in_specs=[pl.BlockSpec((1,) + weights.shape[1:], lambda z: (z, 0, 0, 0))]
        + [pl.BlockSpec((p.shape[0], 1, angles, cross), lambda z: (0, z, 0, 0)) for p in ins],
        out_specs=pl.BlockSpec((lateral, 1, angles, cross), lambda z: (0, z, 0, 0)),
        out_shape=jax.ShapeDtypeStruct((lateral, depth_cells, angles, cross), kind),
        compiler_params=pltpu.CompilerParams(vmem_limit_bytes=32 * 1024 * 1024),
        cost_estimate=pl.CostEstimate(
            flops=200 * planes * depth_cells * angles * cross,
            bytes_accessed=8 * lateral * depth_cells * angles * cross,
            transcendentals=0,
        ),
        name="smooth",
    )(weights, *ins)


def dip_weights(dip_class, coefficients):
    classes, taps = coefficients.shape
    cross = dip_class.shape[-1]
    width = 2 * RY + 1
    padded = jnp.pad(dip_class, ((0, 0), (0, 0), (2 * RY, 2 * RY)), constant_values=-1)
    moved = jnp.stack(
        [padded[:, :, 3 * RY - j : 3 * RY - j + cross] for j in range(width)]
    )
    class_index = jnp.arange(classes, dtype=jnp.int32)
    onehot = (moved[:, :, :, None] == class_index[:, None]).astype(jnp.float32)
    weights = jnp.einsum(
        "qij,jzxqy->zxijy",
        coefficients.reshape(classes, taps // width, width),
        onehot,
        precision=lax.Precision.HIGHEST,
    )
    return weights.reshape(weights.shape[:2] + (taps, cross))


def neighbours(axis):
    count = lax.axis_size(axis)
    up = [(i, i + 1) for i in range(count - 1)]
    return up, [(j, i) for i, j in up]


def halo_of(last, leading):
    up, down = neighbours("depth")
    return lax.ppermute(last, "depth", up), lax.ppermute(leading, "depth", down)


def local(offset_image, dip_class, slant_taper, band_offsets, coefficients):
    offset_count, depth_cells, lateral, cross = offset_image.shape
    angles = slant_taper.shape[0]
    above, below = first_offsets(offset_count)
    right, left = neighbours("gx")
    cols = COLS if lateral % COLS == 0 else lateral

    upper = packed_rows(above[::-1], offset_count)
    lower = packed_rows(below, offset_count)
    group = GROUP if depth_cells % GROUP == 0 else depth_cells
    by_column = jnp.transpose(offset_image, (2, 1, 0, 3))
    last, leading = pack(by_column, upper, lower)
    halos = [
        halo_of(last[first : first + cols], leading[first : first + cols])
        for first in range(0, lateral, cols)
    ]
    matrix = stack_matrix(slant_matrix_of(slant_taper, band_offsets, offset_count), group)
    weights = dip_weights(dip_class, coefficients)
    mine, before, after = [], [], []
    for index, (from_above, from_below) in enumerate(halos):
        part = slant_stack(
            matrix, group, from_above, by_column, from_below, upper, lower, index * cols, cols
        )
        mine.append(part)
        before.append(lax.ppermute(part, "gx", right))
        after.append(lax.ppermute(part, "gx", left))
    parts = before + mine + after
    chunks = [(p, c) for p in range(len(parts)) for c in range(cols)]
    chunks = chunks[lateral - RX : 2 * lateral + RX]
    count = len(mine)
    final = {count - 1, 3 * count - 1} if count > 1 else set()
    early, late = [], []
    for x in range(lateral):
        planes = [(i,) + chunks[x + i] for i in range(2 * RX + 1)]
        early.append([p for p in planes if p[1] not in final])
        late.append([p for p in planes if p[1] in final])
    sizes = (lateral, depth_cells, angles)
    if all(late):
        out = smooth(weights, parts, early, None, *sizes, jnp.float32)
        out = smooth(weights, parts, late, out, *sizes, jnp.bfloat16)
    else:
        out = smooth(weights, parts, [e + l for e, l in zip(early, late)], None, *sizes, jnp.bfloat16)
    return jnp.transpose(out, (2, 1, 0, 3))


def solution(mesh):
    return jax.shard_map(
        local,
        mesh=mesh,
        in_specs=(P(None, "depth", "gx", None), P("depth", "gx", None), P(), P(), P()),
        out_specs=P(None, "depth", "gx", None),
        check_vma=False,
    )
```

```python
import functools

import jax
import jax.numpy as jnp
from jax import lax
from jax.experimental import pallas as pl
from jax.experimental.pallas import tpu as pltpu
from jax.sharding import PartitionSpec as P

R = 16
BAND = 2
RX = 4
RY = 1
COLS = 2
GROUP = 4
ALIGN = 8


def first_offsets(offset_count):
    steep = R - BAND
    above, below = [], []
    for distance in range(1, R + 1):
        up = [h for h in range(offset_count) if -(-steep * h // offset_count) + BAND >= distance]
        down = [h for h in range(offset_count) if steep * h // offset_count + BAND >= distance]
        above.append((up[0] if up else offset_count) // ALIGN * ALIGN)
        below.append((down[0] if down else offset_count) // ALIGN * ALIGN)
    return above, below


def slant_matrix_of(slant_taper, band_offsets, offset_count):
    offset_index = jnp.arange(offset_count, dtype=jnp.int32)
    depth_shift = jnp.floor_divide(band_offsets[:, None] * offset_index[None, :], offset_count)
    reach_index = jnp.arange(slant_taper.shape[2], dtype=jnp.int32) - R
    inside_band = jnp.abs(reach_index[None, None, :] - depth_shift[:, :, None]) <= BAND
    return jnp.where(inside_band, slant_taper, jnp.zeros_like(slant_taper))


def stack_matrix(slant_matrix, group):
    angles, offset_count, reach = slant_matrix.shape
    flat = jnp.swapaxes(slant_matrix, 1, 2).reshape(angles, reach * offset_count)
    rows = [
        jnp.pad(flat, ((0, 0), (z * offset_count, (group - 1 - z) * offset_count)))
        for z in range(group)
    ]
    return jnp.concatenate(rows, axis=0)


def packed_rows(starts, offset_count):
    rows, place = [], 0
    for row, start in enumerate(starts):
        if start < offset_count:
            rows.append((row, start, place))
            place += offset_count - start
    return rows, place


def pack_kernel(upper, lower, image_ref, last_ref, leading_ref):
    depth_cells, offset_count = image_ref.shape[1:3]
    for row, start, place in upper:
        last_ref[0, place : place + offset_count - start, :] = image_ref[
            0, depth_cells - R + row, start:, :
        ]
    for row, start, place in lower:
        leading_ref[0, place : place + offset_count - start, :] = image_ref[0, row, start:, :]


def pack(by_column, upper, lower):
    columns, depth_cells, offset_count, cross = by_column.shape
    sizes = [upper[1], lower[1]]
    return pl.pallas_call(
        functools.partial(pack_kernel, upper[0], lower[0]),
        grid=(columns,),
        in_specs=[pl.BlockSpec((1, depth_cells, offset_count, cross), lambda c: (c, 0, 0, 0))],
        out_specs=[pl.BlockSpec((1, n, cross), lambda c: (c, 0, 0)) for n in sizes],
        out_shape=[jax.ShapeDtypeStruct((columns, n, cross), jnp.bfloat16) for n in sizes],
        compiler_params=pltpu.CompilerParams(vmem_limit_bytes=32 * 1024 * 1024),
        cost_estimate=pl.CostEstimate(
            flops=0, bytes_accessed=4 * columns * sum(sizes) * cross, transcendentals=0
        ),
        name="pack",
    )(by_column)


def stack_kernel(upper, lower, group, matrix_ref, above_ref, own_ref, below_ref, out_ref, planes):
    depth_cells, offset_count, cross = own_ref.shape[1:]
    below_row = R + depth_cells

    @pl.when(pl.program_id(0) == 0)
    def _():
        planes[: R * offset_count, :] = jnp.zeros((R * offset_count, cross), planes.dtype)
        planes[below_row * offset_count :, :] = jnp.zeros((R * offset_count, cross), planes.dtype)

    for row, start, place in upper:
        planes[row * offset_count + start : (row + 1) * offset_count, :] = above_ref[
            0, place : place + offset_count - start, :
        ]
    for row in range(depth_cells):
        planes[(R + row) * offset_count : (R + row + 1) * offset_count, :] = own_ref[0, row]
    for row, start, place in lower:
        first = (below_row + row) * offset_count
        planes[first + start : first + offset_count, :] = below_ref[
            0, place : place + offset_count - start, :
        ]
    tile, depth = matrix_ref.shape
    for z in range(0, depth_cells, group):
        total = jnp.dot(
            matrix_ref[...],
            planes[z * offset_count : z * offset_count + depth, :],
            preferred_element_type=jnp.float32,
        )
        out_ref[0, z // group * tile : (z // group + 1) * tile, :] = total.astype(out_ref.dtype)


def slant_stack(matrix, group, above, by_column, below, upper, lower, first, columns):
    _, depth_cells, offset_count, cross = by_column.shape
    tile, depth = matrix.shape
    rows = depth_cells // group * tile
    return pl.pallas_call(
        functools.partial(stack_kernel, upper[0], lower[0], group),
        grid=(columns,),
        in_specs=[
            pl.BlockSpec((tile, depth), lambda c: (0, 0)),
            pl.BlockSpec((1, upper[1], cross), lambda c: (c, 0, 0)),
            pl.BlockSpec((1, depth_cells, offset_count, cross), lambda c: (c + first, 0, 0, 0)),
            pl.BlockSpec((1, lower[1], cross), lambda c: (c, 0, 0)),
        ],
        out_specs=pl.BlockSpec((1, rows, cross), lambda c: (c, 0, 0)),
        out_shape=jax.ShapeDtypeStruct((columns, rows, cross), jnp.bfloat16),
        scratch_shapes=[pltpu.VMEM(((2 * R + depth_cells) * offset_count, cross), jnp.bfloat16)],
        compiler_params=pltpu.CompilerParams(vmem_limit_bytes=32 * 1024 * 1024),
        cost_estimate=pl.CostEstimate(
            flops=2 * rows * depth * columns * cross,
            bytes_accessed=2 * (tile * depth + columns * (depth + rows) * cross),
            transcendentals=0,
        ),
        name="slant_stack",
    )(matrix, above, by_column, below)


def smooth_kernel(sources, weight_ref, *refs):
    out_ref = refs[-1]
    lateral, _, angles, cross = out_ref.shape
    step = 32 if angles % 32 == 0 else angles
    count = 1 + max(which for planes in sources for _, which, _ in planes)
    for x in range(lateral):
        for first in range(0, angles, step):
            sums = [None] * (2 * RY + 1)
            for i, which, column in sources[x]:
                plane = refs[which][column, 0, first : first + step, :].astype(jnp.float32)
                for j in range(2 * RY + 1):
                    tap = i * (2 * RY + 1) + j
                    term = weight_ref[0, x, tap : tap + 1, :] * plane
                    sums[j] = term if sums[j] is None else sums[j] + term
            total = sums[RY] if sources[x] else jnp.zeros((step, cross), jnp.float32)
            for j in range(2 * RY + 1):
                if j != RY and sources[x]:
                    total = total + pltpu.roll(sums[j], (RY - j) % cross, 1)
            if len(refs) > count + 1:
                total = total + refs[count][x, 0, first : first + step, :]
            out_ref[x, 0, first : first + step, :] = total.astype(out_ref.dtype)


def smooth(weights, parts, sources, partial, lateral, depth_cells, angles, kind):
    cross = weights.shape[-1]
    used = sorted({which for planes in sources for _, which, _ in planes})
    sources = [[(i, used.index(which), column) for i, which, column in planes] for planes in sources]
    ins = [parts[which] for which in used]
    ins = [p.reshape(p.shape[0], depth_cells, angles, cross) for p in ins]
    if partial is not None:
        ins.append(partial)
    planes = sum(len(s) for s in sources)
    return pl.pallas_call(
        functools.partial(smooth_kernel, sources),
        grid=(depth_cells,),
        in_specs=[pl.BlockSpec((1,) + weights.shape[1:], lambda z: (z, 0, 0, 0))]
        + [pl.BlockSpec((p.shape[0], 1, angles, cross), lambda z: (0, z, 0, 0)) for p in ins],
        out_specs=pl.BlockSpec((lateral, 1, angles, cross), lambda z: (0, z, 0, 0)),
        out_shape=jax.ShapeDtypeStruct((lateral, depth_cells, angles, cross), kind),
        compiler_params=pltpu.CompilerParams(vmem_limit_bytes=32 * 1024 * 1024),
        cost_estimate=pl.CostEstimate(
            flops=200 * planes * depth_cells * angles * cross,
            bytes_accessed=8 * lateral * depth_cells * angles * cross,
            transcendentals=0,
        ),
        name="smooth",
    )(weights, *ins)


def dip_weights(dip_class, coefficients):
    classes, taps = coefficients.shape
    cross = dip_class.shape[-1]
    width = 2 * RY + 1
    padded = jnp.pad(dip_class, ((0, 0), (0, 0), (2 * RY, 2 * RY)), constant_values=-1)
    moved = jnp.stack(
        [padded[:, :, 3 * RY - j : 3 * RY - j + cross] for j in range(width)]
    )
    class_index = jnp.arange(classes, dtype=jnp.int32)
    onehot = (moved[:, :, :, None] == class_index[:, None]).astype(jnp.float32)
    weights = jnp.einsum(
        "qij,jzxqy->zxijy",
        coefficients.reshape(classes, taps // width, width),
        onehot,
        precision=lax.Precision.HIGHEST,
    )
    return weights.reshape(weights.shape[:2] + (taps, cross))


def neighbours(axis):
    count = lax.axis_size(axis)
    up = [(i, i + 1) for i in range(count - 1)]
    return up, [(j, i) for i, j in up]


def halos_of(last, leading, cols):
    lateral = last.shape[0]
    chunks = [(last[c : c + cols], leading[c : c + cols]) for c in range(0, lateral, cols)]
    if lax.axis_size("depth") != 4 or last.shape[1] < leading.shape[1]:
        up, down = neighbours("depth")
        return [
            (lax.ppermute(upper, "depth", up), lax.ppermute(lower, "depth", down))
            for upper, lower in chunks
        ]
    place = lax.axis_index("depth")
    rows, columns = ([(1, 0), (2, 3)], [(1, 3), (2, 0)])
    next_rows, next_columns = ([(0, 1), (3, 2)], [(0, 2), (3, 1)])
    pad = last.shape[1] - leading.shape[1]
    relays, results = [], []
    for index, (upper, lower) in enumerate(chunks):
        crossing = jnp.where(place == 1, upper, jnp.pad(lower, ((0, 0), (0, pad), (0, 0))))
        relays.append(lax.ppermute(crossing, "depth", columns if index % 2 else rows))
    for index, (upper, lower) in enumerate(chunks):
        from_above = lax.ppermute(upper, "depth", [(0, 1), (2, 3)])
        from_below = lax.ppermute(lower, "depth", [(1, 0), (3, 2)])
        crossed = lax.ppermute(relays[index], "depth", next_rows if index % 2 else next_columns)
        from_above = jnp.where(place == 2, crossed, from_above)
        from_below = jnp.where(place == 1, crossed[:, : lower.shape[1]], from_below)
        results.append((from_above, from_below))
    return results


def local(offset_image, dip_class, slant_taper, band_offsets, coefficients):
    offset_count, depth_cells, lateral, cross = offset_image.shape
    angles = slant_taper.shape[0]
    above, below = first_offsets(offset_count)
    right, left = neighbours("gx")
    cols = COLS if lateral % COLS == 0 else lateral

    upper = packed_rows(above[::-1], offset_count)
    lower = packed_rows(below, offset_count)
    group = GROUP if depth_cells % GROUP == 0 else depth_cells
    by_column = jnp.transpose(offset_image, (2, 1, 0, 3))
    last, leading = pack(by_column, upper, lower)
    halos = halos_of(last, leading, cols)
    matrix = stack_matrix(slant_matrix_of(slant_taper, band_offsets, offset_count), group)
    weights = dip_weights(dip_class, coefficients)
    matrix, weights = lax.optimization_barrier((matrix, weights))
    mine, before, after = [], [], []
    count = len(halos)
    chunks = [(p, c) for p in range(3 * count) for c in range(cols)]
    chunks = chunks[lateral - RX : 2 * lateral + RX]

    def add_planes(stage, parts, out, kind):
        sources = [
            [(i,) + chunks[x + i] for i in range(2 * RX + 1) if chunks[x + i][0] in stage]
            for x in range(lateral)
        ]
        if not any(sources):
            return out
        return smooth(weights, parts, sources, out, lateral, depth_cells, angles, kind)

    own = set(range(count, 2 * count - 1))
    final = {count - 1, 3 * count - 1}
    out = None
    for index, (from_above, from_below) in enumerate(halos):
        if index == count - 1:
            out = add_planes(own, [None] * count + mine, None, jnp.float32)
            if out is not None:
                out, by_column = lax.optimization_barrier((out, by_column))
        part = slant_stack(
            matrix, group, from_above, by_column, from_below, upper, lower, index * cols, cols
        )
        mine.append(part)
        before.append(lax.ppermute(part, "gx", right))
        after.append(lax.ppermute(part, "gx", left))
    parts = before + mine + after
    out = add_planes(set(range(3 * count)) - own - final, parts, out, jnp.float32)
    out = add_planes(final, parts, out, jnp.bfloat16)
    return jnp.transpose(out, (2, 1, 0, 3))


def solution(mesh):
    return jax.shard_map(
        local,
        mesh=mesh,
        in_specs=(P(None, "depth", "gx", None), P("depth", "gx", None), P(), P(), P()),
        out_specs=P(None, "depth", "gx", None),
        check_vma=False,
    )
```

```python
import functools

import jax
import jax.numpy as jnp
from jax import lax
from jax.experimental import pallas as pl
from jax.experimental.pallas import tpu as pltpu
from jax.sharding import PartitionSpec as P

R = 16
BAND = 2
RX = 4
RY = 1
COLS = 2
GROUP = 4
ALIGN = 8


def first_offsets(offset_count):
    steep = R - BAND
    above, below = [], []
    for distance in range(1, R + 1):
        up = [h for h in range(offset_count) if -(-steep * h // offset_count) + BAND >= distance]
        down = [h for h in range(offset_count) if steep * h // offset_count + BAND >= distance]
        above.append((up[0] if up else offset_count) // ALIGN * ALIGN)
        below.append((down[0] if down else offset_count) // ALIGN * ALIGN)
    return above, below


def slant_matrix_of(slant_taper, band_offsets, offset_count):
    offset_index = jnp.arange(offset_count, dtype=jnp.int32)
    depth_shift = jnp.floor_divide(band_offsets[:, None] * offset_index[None, :], offset_count)
    reach_index = jnp.arange(slant_taper.shape[2], dtype=jnp.int32) - R
    inside_band = jnp.abs(reach_index[None, None, :] - depth_shift[:, :, None]) <= BAND
    return jnp.where(inside_band, slant_taper, jnp.zeros_like(slant_taper))


def stack_matrix(slant_matrix, group):
    angles, offset_count, reach = slant_matrix.shape
    flat = jnp.swapaxes(slant_matrix, 1, 2).reshape(angles, reach * offset_count)
    rows = [
        jnp.pad(flat, ((0, 0), (z * offset_count, (group - 1 - z) * offset_count)))
        for z in range(group)
    ]
    return jnp.concatenate(rows, axis=0)


def packed_rows(starts, offset_count):
    rows, place = [], 0
    for row, start in enumerate(starts):
        if start < offset_count:
            rows.append((row, start, place))
            place += offset_count - start
    return rows, place


def pack_kernel(upper, lower, image_ref, last_ref, leading_ref):
    depth_cells, offset_count = image_ref.shape[1:3]
    for row, start, place in upper:
        last_ref[0, place : place + offset_count - start, :] = image_ref[
            0, depth_cells - R + row, start:, :
        ]
    for row, start, place in lower:
        leading_ref[0, place : place + offset_count - start, :] = image_ref[0, row, start:, :]


def pack(by_column, upper, lower):
    columns, depth_cells, offset_count, cross = by_column.shape
    sizes = [upper[1], lower[1]]
    return pl.pallas_call(
        functools.partial(pack_kernel, upper[0], lower[0]),
        grid=(columns,),
        in_specs=[pl.BlockSpec((1, depth_cells, offset_count, cross), lambda c: (c, 0, 0, 0))],
        out_specs=[pl.BlockSpec((1, n, cross), lambda c: (c, 0, 0)) for n in sizes],
        out_shape=[jax.ShapeDtypeStruct((columns, n, cross), jnp.bfloat16) for n in sizes],
        compiler_params=pltpu.CompilerParams(vmem_limit_bytes=32 * 1024 * 1024),
        cost_estimate=pl.CostEstimate(
            flops=0, bytes_accessed=4 * columns * sum(sizes) * cross, transcendentals=0
        ),
        name="pack",
    )(by_column)


def stack_kernel(upper, lower, group, matrix_ref, above_ref, own_ref, below_ref, out_ref, planes):
    depth_cells, offset_count, cross = own_ref.shape[1:]
    below_row = R + depth_cells

    @pl.when(pl.program_id(0) == 0)
    def _():
        planes[: R * offset_count, :] = jnp.zeros((R * offset_count, cross), planes.dtype)
        planes[below_row * offset_count :, :] = jnp.zeros((R * offset_count, cross), planes.dtype)

    for row, start, place in upper:
        planes[row * offset_count + start : (row + 1) * offset_count, :] = above_ref[
            0, place : place + offset_count - start, :
        ]
    for row in range(depth_cells):
        planes[(R + row) * offset_count : (R + row + 1) * offset_count, :] = own_ref[0, row]
    for row, start, place in lower:
        first = (below_row + row) * offset_count
        planes[first + start : first + offset_count, :] = below_ref[
            0, place : place + offset_count - start, :
        ]
    tile, depth = matrix_ref.shape
    for z in range(0, depth_cells, group):
        total = jnp.dot(
            matrix_ref[...],
            planes[z * offset_count : z * offset_count + depth, :],
            preferred_element_type=jnp.float32,
        )
        out_ref[0, z // group * tile : (z // group + 1) * tile, :] = total.astype(out_ref.dtype)


def slant_stack(matrix, group, above, by_column, below, upper, lower, first, columns):
    _, depth_cells, offset_count, cross = by_column.shape
    tile, depth = matrix.shape
    rows = depth_cells // group * tile
    return pl.pallas_call(
        functools.partial(stack_kernel, upper[0], lower[0], group),
        grid=(columns,),
        in_specs=[
            pl.BlockSpec((tile, depth), lambda c: (0, 0)),
            pl.BlockSpec((1, upper[1], cross), lambda c: (c, 0, 0)),
            pl.BlockSpec((1, depth_cells, offset_count, cross), lambda c: (c + first, 0, 0, 0)),
            pl.BlockSpec((1, lower[1], cross), lambda c: (c, 0, 0)),
        ],
        out_specs=pl.BlockSpec((1, rows, cross), lambda c: (c, 0, 0)),
        out_shape=jax.ShapeDtypeStruct((columns, rows, cross), jnp.bfloat16),
        scratch_shapes=[pltpu.VMEM(((2 * R + depth_cells) * offset_count, cross), jnp.bfloat16)],
        compiler_params=pltpu.CompilerParams(vmem_limit_bytes=32 * 1024 * 1024),
        cost_estimate=pl.CostEstimate(
            flops=2 * rows * depth * columns * cross,
            bytes_accessed=2 * (tile * depth + columns * (depth + rows) * cross),
            transcendentals=0,
        ),
        name="slant_stack",
    )(matrix, above, by_column, below)


def smooth_kernel(sources, weight_ref, *refs):
    out_ref = refs[-1]
    lateral, _, angles, cross = out_ref.shape
    step = 32 if angles % 32 == 0 else angles
    count = 1 + max(which for planes in sources for _, which, _ in planes)
    for x in range(lateral):
        for first in range(0, angles, step):
            sums = [None] * (2 * RY + 1)
            for i, which, column in sources[x]:
                plane = refs[which][column, 0, first : first + step, :].astype(jnp.float32)
                for j in range(2 * RY + 1):
                    tap = i * (2 * RY + 1) + j
                    term = weight_ref[0, x, tap : tap + 1, :] * plane
                    sums[j] = term if sums[j] is None else sums[j] + term
            total = sums[RY] if sources[x] else jnp.zeros((step, cross), jnp.float32)
            for j in range(2 * RY + 1):
                if j != RY and sources[x]:
                    total = total + pltpu.roll(sums[j], (RY - j) % cross, 1)
            if len(refs) > count + 1:
                total = total + refs[count][x, 0, first : first + step, :]
            out_ref[x, 0, first : first + step, :] = total.astype(out_ref.dtype)


def smooth(weights, parts, sources, partial, lateral, depth_cells, angles, kind):
    cross = weights.shape[-1]
    used = sorted({which for planes in sources for _, which, _ in planes})
    sources = [[(i, used.index(which), column) for i, which, column in planes] for planes in sources]
    ins = [parts[which] for which in used]
    ins = [p.reshape(p.shape[0], depth_cells, angles, cross) for p in ins]
    if partial is not None:
        ins.append(partial)
    planes = sum(len(s) for s in sources)
    return pl.pallas_call(
        functools.partial(smooth_kernel, sources),
        grid=(depth_cells,),
        in_specs=[pl.BlockSpec((1,) + weights.shape[1:], lambda z: (z, 0, 0, 0))]
        + [pl.BlockSpec((p.shape[0], 1, angles, cross), lambda z: (0, z, 0, 0)) for p in ins],
        out_specs=pl.BlockSpec((lateral, 1, angles, cross), lambda z: (0, z, 0, 0)),
        out_shape=jax.ShapeDtypeStruct((lateral, depth_cells, angles, cross), kind),
        compiler_params=pltpu.CompilerParams(vmem_limit_bytes=32 * 1024 * 1024),
        cost_estimate=pl.CostEstimate(
            flops=200 * planes * depth_cells * angles * cross,
            bytes_accessed=8 * lateral * depth_cells * angles * cross,
            transcendentals=0,
        ),
        name="smooth",
    )(weights, *ins)


def dip_weights(dip_class, coefficients):
    classes, taps = coefficients.shape
    cross = dip_class.shape[-1]
    width = 2 * RY + 1
    padded = jnp.pad(dip_class, ((0, 0), (0, 0), (2 * RY, 2 * RY)), constant_values=-1)
    moved = jnp.stack(
        [padded[:, :, 3 * RY - j : 3 * RY - j + cross] for j in range(width)]
    )
    class_index = jnp.arange(classes, dtype=jnp.int32)
    onehot = (moved[:, :, :, None] == class_index[:, None]).astype(jnp.float32)
    weights = jnp.einsum(
        "qij,jzxqy->zxijy",
        coefficients.reshape(classes, taps // width, width),
        onehot,
        precision=lax.Precision.HIGHEST,
    )
    return weights.reshape(weights.shape[:2] + (taps, cross))


def neighbours(axis):
    count = lax.axis_size(axis)
    up = [(i, i + 1) for i in range(count - 1)]
    return up, [(j, i) for i, j in up]


def halos_of(last, leading, cols):
    lateral = last.shape[0]
    chunks = [(last[c : c + cols], leading[c : c + cols]) for c in range(0, lateral, cols)]
    if lax.axis_size("depth") != 4 or last.shape[1] < leading.shape[1]:
        up, down = neighbours("depth")
        return [
            (lax.ppermute(upper, "depth", up), lax.ppermute(lower, "depth", down))
            for upper, lower in chunks
        ]
    place = lax.axis_index("depth")
    up, down = neighbours("depth")
    pad = last.shape[1] - leading.shape[1]
    results, relays = [], {}
    for index, (upper, lower) in enumerate(chunks):
        if index % 2:
            crossing = jnp.where(place == 1, upper, jnp.pad(lower, ((0, 0), (0, pad), (0, 0))))
            relays[index] = lax.ppermute(crossing, "depth", [(1, 3), (2, 0)])
    for index, (upper, lower) in enumerate(chunks):
        if index % 2 == 0:
            results.append((lax.ppermute(upper, "depth", up), lax.ppermute(lower, "depth", down)))
            continue
        relayed, upper, lower = lax.optimization_barrier((relays[index], upper, lower))
        crossed = lax.ppermute(relayed, "depth", [(0, 1), (3, 2)])
        from_above = lax.ppermute(upper, "depth", [(0, 1), (2, 3)])
        from_below = lax.ppermute(lower, "depth", [(1, 0), (3, 2)])
        from_above = jnp.where(place == 2, crossed, from_above)
        from_below = jnp.where(place == 1, crossed[:, : lower.shape[1]], from_below)
        results.append((from_above, from_below))
    return results


def local(offset_image, dip_class, slant_taper, band_offsets, coefficients):
    offset_count, depth_cells, lateral, cross = offset_image.shape
    angles = slant_taper.shape[0]
    above, below = first_offsets(offset_count)
    right, left = neighbours("gx")
    cols = COLS if lateral % COLS == 0 else lateral

    upper = packed_rows(above[::-1], offset_count)
    lower = packed_rows(below, offset_count)
    group = GROUP if depth_cells % GROUP == 0 else depth_cells
    by_column = jnp.transpose(offset_image, (2, 1, 0, 3))
    last, leading = pack(by_column, upper, lower)
    halos = halos_of(last, leading, cols)
    matrix = stack_matrix(slant_matrix_of(slant_taper, band_offsets, offset_count), group)
    weights = dip_weights(dip_class, coefficients)
    matrix, weights = lax.optimization_barrier((matrix, weights))
    mine, before, after = [], [], []
    count = len(halos)
    chunks = [(p, c) for p in range(3 * count) for c in range(cols)]
    chunks = chunks[lateral - RX : 2 * lateral + RX]

    def add_planes(stage, parts, out, kind):
        sources = [
            [(i,) + chunks[x + i] for i in range(2 * RX + 1) if chunks[x + i][0] in stage]
            for x in range(lateral)
        ]
        if not any(sources):
            return out
        return smooth(weights, parts, sources, out, lateral, depth_cells, angles, kind)

    own = set(range(count, 2 * count - 1))
    final = {count - 1, 3 * count - 1}
    out = None
    for index, (from_above, from_below) in enumerate(halos):
        if index == count - 1:
            out = add_planes(own, [None] * count + mine, None, jnp.float32)
            if out is not None:
                out, by_column = lax.optimization_barrier((out, by_column))
        part = slant_stack(
            matrix, group, from_above, by_column, from_below, upper, lower, index * cols, cols
        )
        mine.append(part)
        before.append(lax.ppermute(part, "gx", right))
        after.append(lax.ppermute(part, "gx", left))
    parts = before + mine + after
    out = add_planes(set(range(3 * count)) - own - final, parts, out, jnp.float32)
    out = add_planes(final, parts, out, jnp.bfloat16)
    return jnp.transpose(out, (2, 1, 0, 3))


def solution(mesh):
    return jax.shard_map(
        local,
        mesh=mesh,
        in_specs=(P(None, "depth", "gx", None), P("depth", "gx", None), P(), P(), P()),
        out_specs=P(None, "depth", "gx", None),
        check_vma=False,
    )
```

```python
import functools

import jax
import jax.numpy as jnp
from jax import lax
from jax.experimental import pallas as pl
from jax.experimental.pallas import tpu as pltpu
from jax.sharding import PartitionSpec as P

R = 16
BAND = 2
RX = 4
RY = 1
COLS = 2
GROUP = 4
ALIGN = 2


def first_offsets(offset_count):
    steep = R - BAND
    above, below = [], []
    for distance in range(1, R + 1):
        up = [h for h in range(offset_count) if -(-steep * h // offset_count) + BAND >= distance]
        down = [h for h in range(offset_count) if steep * h // offset_count + BAND >= distance]
        above.append((up[0] if up else offset_count) // ALIGN * ALIGN)
        below.append((down[0] if down else offset_count) // ALIGN * ALIGN)
    return above, below


def slant_matrix_of(slant_taper, band_offsets, offset_count):
    offset_index = jnp.arange(offset_count, dtype=jnp.int32)
    depth_shift = jnp.floor_divide(band_offsets[:, None] * offset_index[None, :], offset_count)
    reach_index = jnp.arange(slant_taper.shape[2], dtype=jnp.int32) - R
    inside_band = jnp.abs(reach_index[None, None, :] - depth_shift[:, :, None]) <= BAND
    return jnp.where(inside_band, slant_taper, jnp.zeros_like(slant_taper))


def stack_matrix(slant_matrix, group):
    angles, offset_count, reach = slant_matrix.shape
    flat = jnp.swapaxes(slant_matrix, 1, 2).reshape(angles, reach * offset_count)
    rows = [
        jnp.pad(flat, ((0, 0), (z * offset_count, (group - 1 - z) * offset_count)))
        for z in range(group)
    ]
    return jnp.concatenate(rows, axis=0)


def packed_rows(starts, offset_count):
    rows, place = [], 0
    for row, start in enumerate(starts):
        if start < offset_count:
            rows.append((row, start, place))
            place += offset_count - start
    return rows, place


def pack_kernel(upper, lower, image_ref, last_ref, leading_ref):
    depth_cells, offset_count = image_ref.shape[1:3]
    for row, start, place in upper:
        last_ref[0, place : place + offset_count - start, :] = image_ref[
            0, depth_cells - R + row, start:, :
        ]
    for row, start, place in lower:
        leading_ref[0, place : place + offset_count - start, :] = image_ref[0, row, start:, :]


def pack(by_column, upper, lower, first, columns):
    _, depth_cells, offset_count, cross = by_column.shape
    sizes = [upper[1], lower[1]]
    return pl.pallas_call(
        functools.partial(pack_kernel, upper[0], lower[0]),
        grid=(columns,),
        in_specs=[
            pl.BlockSpec((1, depth_cells, offset_count, cross), lambda c: (c + first, 0, 0, 0))
        ],
        out_specs=[pl.BlockSpec((1, n, cross), lambda c: (c, 0, 0)) for n in sizes],
        out_shape=[jax.ShapeDtypeStruct((columns, n, cross), jnp.bfloat16) for n in sizes],
        compiler_params=pltpu.CompilerParams(vmem_limit_bytes=32 * 1024 * 1024),
        cost_estimate=pl.CostEstimate(
            flops=0, bytes_accessed=4 * columns * sum(sizes) * cross, transcendentals=0
        ),
        name="pack",
    )(by_column)


def stack_kernel(upper, lower, group, matrix_ref, above_ref, own_ref, below_ref, out_ref, planes):
    depth_cells, offset_count, cross = own_ref.shape[1:]
    below_row = R + depth_cells

    @pl.when(pl.program_id(0) == 0)
    def _():
        planes[: R * offset_count, :] = jnp.zeros((R * offset_count, cross), planes.dtype)
        planes[below_row * offset_count :, :] = jnp.zeros((R * offset_count, cross), planes.dtype)

    for row, start, place in upper:
        planes[row * offset_count + start : (row + 1) * offset_count, :] = above_ref[
            0, place : place + offset_count - start, :
        ]
    for row in range(depth_cells):
        planes[(R + row) * offset_count : (R + row + 1) * offset_count, :] = own_ref[0, row]
    for row, start, place in lower:
        first = (below_row + row) * offset_count
        planes[first + start : first + offset_count, :] = below_ref[
            0, place : place + offset_count - start, :
        ]
    tile, depth = matrix_ref.shape
    for z in range(0, depth_cells, group):
        total = jnp.dot(
            matrix_ref[...],
            planes[z * offset_count : z * offset_count + depth, :],
            preferred_element_type=jnp.float32,
        )
        out_ref[0, z // group * tile : (z // group + 1) * tile, :] = total.astype(out_ref.dtype)


def slant_stack(matrix, group, above, by_column, below, upper, lower, first, columns):
    _, depth_cells, offset_count, cross = by_column.shape
    tile, depth = matrix.shape
    rows = depth_cells // group * tile
    return pl.pallas_call(
        functools.partial(stack_kernel, upper[0], lower[0], group),
        grid=(columns,),
        in_specs=[
            pl.BlockSpec((tile, depth), lambda c: (0, 0)),
            pl.BlockSpec((1, upper[1], cross), lambda c: (c, 0, 0)),
            pl.BlockSpec((1, depth_cells, offset_count, cross), lambda c: (c + first, 0, 0, 0)),
            pl.BlockSpec((1, lower[1], cross), lambda c: (c, 0, 0)),
        ],
        out_specs=pl.BlockSpec((1, rows, cross), lambda c: (c, 0, 0)),
        out_shape=jax.ShapeDtypeStruct((columns, rows, cross), jnp.bfloat16),
        scratch_shapes=[pltpu.VMEM(((2 * R + depth_cells) * offset_count, cross), jnp.bfloat16)],
        compiler_params=pltpu.CompilerParams(vmem_limit_bytes=32 * 1024 * 1024),
        cost_estimate=pl.CostEstimate(
            flops=2 * rows * depth * columns * cross,
            bytes_accessed=2 * (tile * depth + columns * (depth + rows) * cross),
            transcendentals=0,
        ),
        name="slant_stack",
    )(matrix, above, by_column, below)


def smooth_kernel(sources, weight_ref, *refs):
    out_ref = refs[-1]
    lateral, _, angles, cross = out_ref.shape
    step = 32 if angles % 32 == 0 else angles
    count = 1 + max(which for planes in sources for _, which, _ in planes)
    for x in range(lateral):
        for first in range(0, angles, step):
            sums = [None] * (2 * RY + 1)
            for i, which, column in sources[x]:
                plane = refs[which][column, 0, first : first + step, :].astype(jnp.float32)
                for j in range(2 * RY + 1):
                    tap = i * (2 * RY + 1) + j
                    term = weight_ref[0, x, tap : tap + 1, :] * plane
                    sums[j] = term if sums[j] is None else sums[j] + term
            total = sums[RY] if sources[x] else jnp.zeros((step, cross), jnp.float32)
            for j in range(2 * RY + 1):
                if j != RY and sources[x]:
                    total = total + pltpu.roll(sums[j], (RY - j) % cross, 1)
            if len(refs) > count + 1:
                total = total + refs[count][x, 0, first : first + step, :]
            out_ref[x, 0, first : first + step, :] = total.astype(out_ref.dtype)


def smooth(weights, parts, sources, partial, lateral, depth_cells, angles, kind):
    cross = weights.shape[-1]
    used = sorted({which for planes in sources for _, which, _ in planes})
    sources = [[(i, used.index(which), column) for i, which, column in planes] for planes in sources]
    ins = [parts[which] for which in used]
    ins = [p.reshape(p.shape[0], depth_cells, angles, cross) for p in ins]
    if partial is not None:
        ins.append(partial)
    planes = sum(len(s) for s in sources)
    return pl.pallas_call(
        functools.partial(smooth_kernel, sources),
        grid=(depth_cells,),
        in_specs=[pl.BlockSpec((1,) + weights.shape[1:], lambda z: (z, 0, 0, 0))]
        + [pl.BlockSpec((p.shape[0], 1, angles, cross), lambda z: (0, z, 0, 0)) for p in ins],
        out_specs=pl.BlockSpec((lateral, 1, angles, cross), lambda z: (0, z, 0, 0)),
        out_shape=jax.ShapeDtypeStruct((lateral, depth_cells, angles, cross), kind),
        compiler_params=pltpu.CompilerParams(vmem_limit_bytes=32 * 1024 * 1024),
        cost_estimate=pl.CostEstimate(
            flops=200 * planes * depth_cells * angles * cross,
            bytes_accessed=8 * lateral * depth_cells * angles * cross,
            transcendentals=0,
        ),
        name="smooth",
    )(weights, *ins)


def dip_weights(dip_class, coefficients):
    classes, taps = coefficients.shape
    cross = dip_class.shape[-1]
    width = 2 * RY + 1
    padded = jnp.pad(dip_class, ((0, 0), (0, 0), (2 * RY, 2 * RY)), constant_values=-1)
    moved = jnp.stack(
        [padded[:, :, 3 * RY - j : 3 * RY - j + cross] for j in range(width)]
    )
    class_index = jnp.arange(classes, dtype=jnp.int32)
    onehot = (moved[:, :, :, None] == class_index[:, None]).astype(jnp.float32)
    weights = jnp.einsum(
        "qij,jzxqy->zxijy",
        coefficients.reshape(classes, taps // width, width),
        onehot,
        precision=lax.Precision.HIGHEST,
    )
    return weights.reshape(weights.shape[:2] + (taps, cross))


def neighbours(axis):
    count = lax.axis_size(axis)
    up = [(i, i + 1) for i in range(count - 1)]
    return up, [(j, i) for i, j in up]


def halos_of(chunks):
    last, leading = chunks[0]
    if lax.axis_size("depth") != 4 or last.shape[1] < leading.shape[1]:
        up, down = neighbours("depth")
        return [
            (lax.ppermute(upper, "depth", up), lax.ppermute(lower, "depth", down))
            for upper, lower in chunks
        ]
    place = lax.axis_index("depth")
    up, down = neighbours("depth")
    pad = last.shape[1] - leading.shape[1]
    results, relays = [], {}
    for index, (upper, lower) in enumerate(chunks):
        if index % 2:
            crossing = jnp.where(place == 1, upper, jnp.pad(lower, ((0, 0), (0, pad), (0, 0))))
            relays[index] = lax.ppermute(crossing, "depth", [(1, 3), (2, 0)])
    for index, (upper, lower) in enumerate(chunks):
        if index % 2 == 0:
            results.append((lax.ppermute(upper, "depth", up), lax.ppermute(lower, "depth", down)))
            continue
        relayed, upper, lower = lax.optimization_barrier((relays[index], upper, lower))
        crossed = lax.ppermute(relayed, "depth", [(0, 1), (3, 2)])
        from_above = lax.ppermute(upper, "depth", [(0, 1), (2, 3)])
        from_below = lax.ppermute(lower, "depth", [(1, 0), (3, 2)])
        from_above = jnp.where(place == 2, crossed, from_above)
        from_below = jnp.where(place == 1, crossed[:, : lower.shape[1]], from_below)
        results.append((from_above, from_below))
    return results


def local(offset_image, dip_class, slant_taper, band_offsets, coefficients):
    offset_count, depth_cells, lateral, cross = offset_image.shape
    angles = slant_taper.shape[0]
    above, below = first_offsets(offset_count)
    right, left = neighbours("gx")
    cols = COLS if lateral % COLS == 0 else lateral

    upper = packed_rows(above[::-1], offset_count)
    lower = packed_rows(below, offset_count)
    group = GROUP if depth_cells % GROUP == 0 else depth_cells
    by_column = jnp.transpose(offset_image, (2, 1, 0, 3))
    halos = halos_of(
        [pack(by_column, upper, lower, first, cols) for first in range(0, lateral, cols)]
    )
    matrix = stack_matrix(slant_matrix_of(slant_taper, band_offsets, offset_count), group)
    weights = dip_weights(dip_class, coefficients)
    matrix, weights = lax.optimization_barrier((matrix, weights))
    mine, before, after = [], [], []
    count = len(halos)
    chunks = [(p, c) for p in range(3 * count) for c in range(cols)]
    chunks = chunks[lateral - RX : 2 * lateral + RX]

    def add_planes(stage, parts, out, kind):
        sources = [
            [(i,) + chunks[x + i] for i in range(2 * RX + 1) if chunks[x + i][0] in stage]
            for x in range(lateral)
        ]
        if not any(sources):
            return out
        return smooth(weights, parts, sources, out, lateral, depth_cells, angles, kind)

    own = set(range(count, 2 * count - 1))
    final = {count - 1, 3 * count - 1}
    out = None
    for index, (from_above, from_below) in enumerate(halos):
        if index == count - 1:
            out = add_planes(own, [None] * count + mine, None, jnp.float32)
            if out is not None:
                out, by_column = lax.optimization_barrier((out, by_column))
        part = slant_stack(
            matrix, group, from_above, by_column, from_below, upper, lower, index * cols, cols
        )
        mine.append(part)
        before.append(lax.ppermute(part, "gx", right))
        after.append(lax.ppermute(part, "gx", left))
    parts = before + mine + after
    out = add_planes(set(range(3 * count)) - own - final, parts, out, jnp.float32)
    out = add_planes(final, parts, out, jnp.bfloat16)
    return jnp.transpose(out, (2, 1, 0, 3))


def solution(mesh):
    return jax.shard_map(
        local,
        mesh=mesh,
        in_specs=(P(None, "depth", "gx", None), P("depth", "gx", None), P(), P(), P()),
        out_specs=P(None, "depth", "gx", None),
        check_vma=False,
    )
```

```python
import functools

import jax
import jax.numpy as jnp
from jax import lax
from jax.experimental import pallas as pl
from jax.experimental.pallas import tpu as pltpu
from jax.sharding import PartitionSpec as P

R = 16
BAND = 2
RX = 4
RY = 1
COLS = 2
GROUP = 4
ALIGN = 2


def first_offsets(offset_count):
    steep = R - BAND
    above, below = [], []
    for distance in range(1, R + 1):
        up = [h for h in range(offset_count) if -(-steep * h // offset_count) + BAND >= distance]
        down = [h for h in range(offset_count) if steep * h // offset_count + BAND >= distance]
        above.append((up[0] if up else offset_count) // ALIGN * ALIGN)
        below.append((down[0] if down else offset_count) // ALIGN * ALIGN)
    return above, below


def slant_matrix_of(slant_taper, band_offsets, offset_count):
    offset_index = jnp.arange(offset_count, dtype=jnp.int32)
    depth_shift = jnp.floor_divide(band_offsets[:, None] * offset_index[None, :], offset_count)
    reach_index = jnp.arange(slant_taper.shape[2], dtype=jnp.int32) - R
    inside_band = jnp.abs(reach_index[None, None, :] - depth_shift[:, :, None]) <= BAND
    return jnp.where(inside_band, slant_taper, jnp.zeros_like(slant_taper))


def stack_matrix(slant_matrix, group):
    angles, offset_count, reach = slant_matrix.shape
    flat = jnp.swapaxes(slant_matrix, 1, 2).reshape(angles, reach * offset_count)
    rows = [
        jnp.pad(flat, ((0, 0), (z * offset_count, (group - 1 - z) * offset_count)))
        for z in range(group)
    ]
    return jnp.concatenate(rows, axis=0)


def packed_rows(starts, offset_count):
    rows, place = [], 0
    for row, start in enumerate(starts):
        if start < offset_count:
            rows.append((row, start, place))
            place += offset_count - start
    return rows, place


def pack_kernel(upper, lower, image_ref, last_ref, leading_ref):
    depth_cells, offset_count = image_ref.shape[1:3]
    for row, start, place in upper:
        last_ref[0, place : place + offset_count - start, :] = image_ref[
            0, depth_cells - R + row, start:, :
        ]
    for row, start, place in lower:
        leading_ref[0, place : place + offset_count - start, :] = image_ref[0, row, start:, :]


def pack(by_column, upper, lower, first, columns):
    _, depth_cells, offset_count, cross = by_column.shape
    sizes = [upper[1], lower[1]]
    return pl.pallas_call(
        functools.partial(pack_kernel, upper[0], lower[0]),
        grid=(columns,),
        in_specs=[
            pl.BlockSpec((1, depth_cells, offset_count, cross), lambda c: (c + first, 0, 0, 0))
        ],
        out_specs=[pl.BlockSpec((1, n, cross), lambda c: (c, 0, 0)) for n in sizes],
        out_shape=[jax.ShapeDtypeStruct((columns, n, cross), jnp.bfloat16) for n in sizes],
        compiler_params=pltpu.CompilerParams(vmem_limit_bytes=32 * 1024 * 1024),
        cost_estimate=pl.CostEstimate(
            flops=0, bytes_accessed=4 * columns * sum(sizes) * cross, transcendentals=0
        ),
        name="pack",
    )(by_column)


def stack_kernel(upper, lower, group, matrix_ref, above_ref, own_ref, below_ref, out_ref, planes):
    depth_cells, offset_count, cross = own_ref.shape[1:]
    below_row = R + depth_cells

    @pl.when(pl.program_id(0) == 0)
    def _():
        planes[: R * offset_count, :] = jnp.zeros((R * offset_count, cross), planes.dtype)
        planes[below_row * offset_count :, :] = jnp.zeros((R * offset_count, cross), planes.dtype)

    for row, start, place in upper:
        planes[row * offset_count + start : (row + 1) * offset_count, :] = above_ref[
            0, place : place + offset_count - start, :
        ]
    for row in range(depth_cells):
        planes[(R + row) * offset_count : (R + row + 1) * offset_count, :] = own_ref[0, row]
    for row, start, place in lower:
        first = (below_row + row) * offset_count
        planes[first + start : first + offset_count, :] = below_ref[
            0, place : place + offset_count - start, :
        ]
    tile, depth = matrix_ref.shape
    for z in range(0, depth_cells, group):
        total = jnp.dot(
            matrix_ref[...],
            planes[z * offset_count : z * offset_count + depth, :],
            preferred_element_type=jnp.float32,
        )
        out_ref[0, z // group * tile : (z // group + 1) * tile, :] = total.astype(out_ref.dtype)


def slant_stack(matrix, group, above, by_column, below, upper, lower, first, columns):
    _, depth_cells, offset_count, cross = by_column.shape
    tile, depth = matrix.shape
    rows = depth_cells // group * tile
    return pl.pallas_call(
        functools.partial(stack_kernel, upper[0], lower[0], group),
        grid=(columns,),
        in_specs=[
            pl.BlockSpec((tile, depth), lambda c: (0, 0)),
            pl.BlockSpec((1, upper[1], cross), lambda c: (c, 0, 0)),
            pl.BlockSpec((1, depth_cells, offset_count, cross), lambda c: (c + first, 0, 0, 0)),
            pl.BlockSpec((1, lower[1], cross), lambda c: (c, 0, 0)),
        ],
        out_specs=pl.BlockSpec((1, rows, cross), lambda c: (c, 0, 0)),
        out_shape=jax.ShapeDtypeStruct((columns, rows, cross), jnp.bfloat16),
        scratch_shapes=[pltpu.VMEM(((2 * R + depth_cells) * offset_count, cross), jnp.bfloat16)],
        compiler_params=pltpu.CompilerParams(vmem_limit_bytes=32 * 1024 * 1024),
        cost_estimate=pl.CostEstimate(
            flops=2 * rows * depth * columns * cross,
            bytes_accessed=2 * (tile * depth + columns * (depth + rows) * cross),
            transcendentals=0,
        ),
        name="slant_stack",
    )(matrix, above, by_column, below)


def smooth_kernel(sources, weight_ref, *refs):
    out_ref = refs[-1]
    lateral, _, angles, cross = out_ref.shape
    step = 32 if angles % 32 == 0 else angles
    count = 1 + max(which for planes in sources for _, which, _ in planes)
    for x in range(lateral):
        for first in range(0, angles, step):
            sums = [None] * (2 * RY + 1)
            for i, which, column in sources[x]:
                plane = refs[which][column, 0, first : first + step, :].astype(jnp.float32)
                for j in range(2 * RY + 1):
                    tap = i * (2 * RY + 1) + j
                    term = weight_ref[0, x, tap : tap + 1, :] * plane
                    sums[j] = term if sums[j] is None else sums[j] + term
            total = sums[RY] if sources[x] else jnp.zeros((step, cross), jnp.float32)
            for j in range(2 * RY + 1):
                if j != RY and sources[x]:
                    total = total + pltpu.roll(sums[j], (RY - j) % cross, 1)
            if len(refs) > count + 1:
                total = total + refs[count][x, 0, first : first + step, :]
            out_ref[x, 0, first : first + step, :] = total.astype(out_ref.dtype)


def smooth(weights, parts, sources, partial, lateral, depth_cells, angles, kind):
    cross = weights.shape[-1]
    used = sorted({which for planes in sources for _, which, _ in planes})
    sources = [[(i, used.index(which), column) for i, which, column in planes] for planes in sources]
    ins = [parts[which] for which in used]
    ins = [p.reshape(p.shape[0], depth_cells, angles, cross) for p in ins]
    if partial is not None:
        ins.append(partial)
    planes = sum(len(s) for s in sources)
    return pl.pallas_call(
        functools.partial(smooth_kernel, sources),
        grid=(depth_cells,),
        in_specs=[pl.BlockSpec((1,) + weights.shape[1:], lambda z: (z, 0, 0, 0))]
        + [pl.BlockSpec((p.shape[0], 1, angles, cross), lambda z: (0, z, 0, 0)) for p in ins],
        out_specs=pl.BlockSpec((lateral, 1, angles, cross), lambda z: (0, z, 0, 0)),
        out_shape=jax.ShapeDtypeStruct((lateral, depth_cells, angles, cross), kind),
        compiler_params=pltpu.CompilerParams(vmem_limit_bytes=32 * 1024 * 1024),
        cost_estimate=pl.CostEstimate(
            flops=200 * planes * depth_cells * angles * cross,
            bytes_accessed=8 * lateral * depth_cells * angles * cross,
            transcendentals=0,
        ),
        name="smooth",
    )(weights, *ins)


def dip_weights(dip_class, coefficients):
    classes, taps = coefficients.shape
    cross = dip_class.shape[-1]
    width = 2 * RY + 1
    padded = jnp.pad(dip_class, ((0, 0), (0, 0), (2 * RY, 2 * RY)), constant_values=-1)
    moved = jnp.stack(
        [padded[:, :, 3 * RY - j : 3 * RY - j + cross] for j in range(width)]
    )
    class_index = jnp.arange(classes, dtype=jnp.int32)
    onehot = (moved[:, :, :, None] == class_index[:, None]).astype(jnp.float32)
    weights = jnp.einsum(
        "qij,jzxqy->zxijy",
        coefficients.reshape(classes, taps // width, width),
        onehot,
        precision=lax.Precision.HIGHEST,
    )
    return weights.reshape(weights.shape[:2] + (taps, cross))


def neighbours(axis):
    count = lax.axis_size(axis)
    up = [(i, i + 1) for i in range(count - 1)]
    return up, [(j, i) for i, j in up]


def halos_of(chunks):
    last, leading = chunks[0]
    if lax.axis_size("depth") != 4 or last.shape[1] < leading.shape[1]:
        up, down = neighbours("depth")
        return [
            (lax.ppermute(upper, "depth", up), lax.ppermute(lower, "depth", down))
            for upper, lower in chunks
        ]
    place = lax.axis_index("depth")
    up, down = neighbours("depth")
    pad = last.shape[1] - leading.shape[1]
    results, relays = [], {}
    for index, (upper, lower) in enumerate(chunks):
        if index % 2:
            crossing = jnp.where(place == 1, upper, jnp.pad(lower, ((0, 0), (0, pad), (0, 0))))
            relays[index] = lax.ppermute(crossing, "depth", [(1, 3), (2, 0)])
    for index, (upper, lower) in enumerate(chunks):
        if index % 2 == 0:
            results.append((lax.ppermute(upper, "depth", up), lax.ppermute(lower, "depth", down)))
            continue
        relayed, upper, lower = lax.optimization_barrier((relays[index], upper, lower))
        crossed = lax.ppermute(relayed, "depth", [(0, 1), (3, 2)])
        from_above = lax.ppermute(upper, "depth", [(0, 1), (2, 3)])
        from_below = lax.ppermute(lower, "depth", [(1, 0), (3, 2)])
        from_above = jnp.where(place == 2, crossed, from_above)
        from_below = jnp.where(place == 1, crossed[:, : lower.shape[1]], from_below)
        results.append((from_above, from_below))
    return results


def local(offset_image, dip_class, slant_taper, band_offsets, coefficients):
    offset_count, depth_cells, lateral, cross = offset_image.shape
    angles = slant_taper.shape[0]
    above, below = first_offsets(offset_count)
    right, left = neighbours("gx")
    cols = COLS if lateral % COLS == 0 else lateral

    upper = packed_rows(above[::-1], offset_count)
    lower = packed_rows(below, offset_count)
    group = GROUP if depth_cells % GROUP == 0 else depth_cells
    by_column = jnp.transpose(offset_image, (2, 1, 0, 3))
    halos = halos_of(
        [pack(by_column, upper, lower, first, cols) for first in range(0, lateral, cols)]
    )
    matrix = stack_matrix(slant_matrix_of(slant_taper, band_offsets, offset_count), group)
    weights = dip_weights(dip_class, coefficients)
    mine, before, after = [], [], []
    count = len(halos)
    chunks = [(p, c) for p in range(3 * count) for c in range(cols)]
    chunks = chunks[lateral - RX : 2 * lateral + RX]

    def add_planes(stage, parts, out, kind):
        sources = [
            [(i,) + chunks[x + i] for i in range(2 * RX + 1) if chunks[x + i][0] in stage]
            for x in range(lateral)
        ]
        if not any(sources):
            return out
        return smooth(weights, parts, sources, out, lateral, depth_cells, angles, kind)

    own = set(range(count, 2 * count - 1))
    final = {count - 1, 3 * count - 1}
    out = None
    for index, (from_above, from_below) in enumerate(halos):
        if index == count - 1:
            out = add_planes(own, [None] * count + mine, None, jnp.float32)
            if out is not None:
                out, by_column = lax.optimization_barrier((out, by_column))
        part = slant_stack(
            matrix, group, from_above, by_column, from_below, upper, lower, index * cols, cols
        )
        mine.append(part)
        before.append(lax.ppermute(part, "gx", right))
        after.append(lax.ppermute(part, "gx", left))
    parts = before + mine + after
    out = add_planes(set(range(3 * count)) - own - final, parts, out, jnp.float32)
    out = add_planes(final, parts, out, jnp.bfloat16)
    return jnp.transpose(out, (2, 1, 0, 3))


def solution(mesh):
    return jax.shard_map(
        local,
        mesh=mesh,
        in_specs=(P(None, "depth", "gx", None), P("depth", "gx", None), P(), P(), P()),
        out_specs=P(None, "depth", "gx", None),
        check_vma=False,
    )
```
